1024 devices in a mesh: blk: 64 (over y, x, z_hi), grp: 16 (over z_lo, core).
Axes of the slice: x: 4, y: 4, z: 32 (z_hi: 4, z_lo: 8; z = z_hi * 8 + z_lo), core: 2. Of those that a mesh axis runs over, the one named last changes fastest.
Arguments:
- image_embed: bfloat16 [262144, 1152], P(('blk', 'grp')), may hold values from -0.19921875 to 0.19921875
- text_embed: bfloat16 [262144, 1152], P(('blk', 'grp')), may hold values from -0.19921875 to 0.19921875
- log_temp: float32 [1], replicated, may hold values from 1.4 to 2.1
- logit_bias: float32 [1], replicated, may hold values from -5 to -3
Outputs:
- loss_rows: float32 [262144], P(('blk', 'grp'))
- grad_image: bfloat16 [262144, 1152], P(('blk', 'grp'))
- grad_text: bfloat16 [262144, 1152], P(('blk', 'grp'))
The draws below stay inside these ranges and needn't reach their ends.
All inputs are finite; a program needn't handle non-finite values.
Results may differ from the reference program's by a relative error of at most 0.0054.
Values may be sent and summed in bfloat16 or wider, within the bound.
No kernel may reach another device: no remote copies, remote signals or barrier semaphores. Data moves between devices by JAX's collectives and lax.ppermute only.
A program may use at most 32 MiB of HBM per device.

```python
import jax
import jax.numpy as jnp
from jax import lax

D = 1152
ROWS = 256
SHIFTS = 2
TOKENS = 262144
N_GRP = 16


def steps_of(key, extent, cuts, least, top_value):
    loudness, own = 1.0, jax.random.fold_in(key, 6)
    for position, parts in cuts:
        draws = jnp.exp(jax.random.uniform(jax.random.fold_in(own, position), (parts,), jnp.float32, least / len(cuts), top_value / len(cuts)))
        loudness = loudness * jnp.repeat(draws, extent[position] // parts).reshape([-1 if axis == position else 1 for axis in range(len(extent))])
    return loudness


def scatter_about(rng, dims, deviation, bound, cuts=(), kind=jnp.bfloat16):
    loudness = steps_of(rng, dims, cuts, -0.22, 0.18) if cuts else 1.0
    drawn = jax.random.normal(rng, dims, jnp.float32) * deviation * loudness
    return jnp.minimum(jnp.maximum(drawn, -bound), bound).astype(kind)


def setup_inputs(seed: int = 0) -> dict:
    keys = jax.random.split(jax.random.key(seed), 5)
    return {
        "image_embed": scatter_about(keys[0], (TOKENS, D), 0.03, 0.19921875, ((0, 1024),)),
        "text_embed": scatter_about(keys[1], (TOKENS, D), 0.03, 0.19921875, ((0, 1024),)),
        "log_temp": jnp.clip(jax.random.uniform(keys[2], (1,), jnp.float32, 1.4, 2.1), 1.4, 2.1),
        "logit_bias": jnp.clip(jax.random.uniform(keys[3], (1,), jnp.float32, -5.0, -3.0), -5.0, -3.0),
    }


def normalize(embed):
    wide = embed.astype(jnp.float32)
    inv = 1.0 / jnp.sqrt(lax.optimization_barrier(jnp.sum(wide * wide, axis=-1, keepdims=True)) + 1e-06)
    unit = wide * inv
    return (inv, unit, unit.astype(jnp.bfloat16))

def unnormalize(inv, unit, grad):
    return (inv * (grad - unit * lax.optimization_barrier(jnp.sum(unit * grad, axis=-1, keepdims=True)))).astype(jnp.bfloat16)

def reference(image_embed, text_embed, log_temp, logit_bias):
    nblk = image_embed.shape[0] // (ROWS * N_GRP)
    shape4 = (nblk, N_GRP, ROWS, D)
    inv_img, unit_img, img_hat = normalize(image_embed.reshape(shape4))
    inv_txt, unit_txt, txt_hat = normalize(text_embed.reshape(shape4))
    scale = jnp.exp(log_temp[0])
    eye = jnp.eye(ROWS, dtype=jnp.float32)
    img32 = img_hat.astype(jnp.float32)
    loss = jnp.zeros((nblk, N_GRP, ROWS), jnp.float32)
    d_img = jnp.zeros(shape4, jnp.float32)
    d_txt = jnp.zeros(shape4, jnp.float32)
    for s in range(-SHIFTS, SHIFTS + 1):
        other = jnp.roll(txt_hat, -s, axis=0).astype(jnp.float32)
        logits = scale * jnp.einsum('bgid,bgjd->bgij', img32, other) + logit_bias[0]
        if s == 0:
            sign = 2.0 * eye - 1.0
            target = eye
        else:
            sign = -jnp.ones_like(eye)
            target = jnp.zeros_like(eye)
        loss = loss + lax.optimization_barrier(jnp.sum(jax.nn.softplus(-sign * logits), axis=-1))
        weights = (jax.nn.sigmoid(logits) - target).astype(jnp.bfloat16).astype(jnp.float32)
        d_img = d_img + scale * jnp.einsum('bgij,bgjd->bgid', weights, other)
        part = scale * jnp.einsum('bgij,bgid->bgjd', weights, img32)
        d_txt = d_txt + jnp.roll(part, s, axis=0)
    loss_rows = loss.reshape(-1)
    grad_image = unnormalize(inv_img, unit_img, d_img).reshape(-1, D)
    grad_text = unnormalize(inv_txt, unit_txt, d_txt).reshape(-1, D)
    return (loss_rows, grad_image, grad_text)
```

```python
import jax
import jax.numpy as jnp
from jax import lax
from jax.sharding import PartitionSpec as P

CHUNKS = 2


def move(block, target):
    size = lax.axis_size("blk")
    return lax.ppermute(block, "blk", [(b, target(b) % size) for b in range(size)])


def image_partner(b):
    return b ^ 1


def text_partner(b):
    return b - 1 if b % 2 == 0 else b + 1


def text_relay(b):
    return b - 4 if b % 2 == 0 else b + 4


def image_relay(b):
    return b + 4 if b % 2 == 0 else b - 4


def normalize(embed):
    wide = embed.astype(jnp.float32)
    inv = 1.0 / jnp.sqrt(jnp.sum(wide * wide, axis=-1, keepdims=True) + 1e-06)
    unit = wide * inv
    return (inv, unit, unit.astype(jnp.bfloat16))


def project(inv, unit, grad):
    return inv * (grad - unit * jnp.sum(unit * grad, axis=-1, keepdims=True))


def dot(a, b):
    return jnp.dot(a, b, preferred_element_type=jnp.float32)


def on_device(image_embed, text_embed, log_temp, logit_bias):
    rows = image_embed.shape[0]
    cut = rows // CHUNKS
    scale = jnp.exp(log_temp[0])
    bias = logit_bias[0]

    img_parts, txt_parts = [], []
    for k in range(CHUNKS):
        img_parts.append(move(image_embed[k * cut : (k + 1) * cut], image_partner))
        txt_parts.append(move(text_embed[k * cut : (k + 1) * cut], text_partner))

    def logits_of(img, txt):
        return scale * dot(img, txt.T) + bias

    def summed(logits):
        return jnp.sum(jax.nn.softplus(logits), axis=-1)

    def weigh(logits):
        return jax.nn.sigmoid(logits).astype(jnp.bfloat16)

    inv_i0, unit_i0, i0 = normalize(image_embed)
    inv_t0, unit_t0, t0 = normalize(text_embed)
    eye = jnp.eye(rows, dtype=jnp.float32)
    logits = logits_of(i0, t0)
    loss0 = jnp.sum(jax.nn.softplus((1.0 - 2.0 * eye) * logits), axis=-1)
    w00 = (jax.nn.sigmoid(logits) - eye).astype(jnp.bfloat16)

    img_norm = [normalize(p) for p in img_parts]
    txt_norm = [normalize(p) for p in txt_parts]
    ti_parts = [move(n[2], text_relay) for n in txt_norm]
    ii_parts = [move(n[2], image_relay) for n in img_norm]
    inv_i1, unit_i1, i1 = (jnp.concatenate(v) for v in zip(*img_norm))
    inv_t1, unit_t1, t1 = (jnp.concatenate(v) for v in zip(*txt_norm))

    l01 = logits_of(i0, t1)
    l10 = logits_of(i1, t0)
    l11 = logits_of(i1, t1)
    w01, w10, w11 = weigh(l01), weigh(l10), weigh(l11)
    loss0 = loss0 + summed(l01)
    loss1 = summed(l10) + summed(l11)
    di1 = dot(w10, t0) + dot(w11, t1)
    dt1 = dot(w01.T, i0) + dot(w11.T, i1)

    tr = jnp.concatenate(ti_parts)
    ir = jnp.concatenate(ii_parts)
    l1r = logits_of(i1, tr)
    lr1 = logits_of(ir, t1)
    loss1 = loss1 + summed(l1r)
    di1 = di1 + dot(weigh(l1r), tr)
    dt1 = dt1 + dot(weigh(lr1).T, ir)

    gi1 = project(inv_i1, unit_i1, scale * di1).astype(jnp.bfloat16)
    gt1 = project(inv_t1, unit_t1, scale * dt1).astype(jnp.bfloat16)
    gi = move(gi1, image_partner)
    gt = move(gt1, text_partner)
    loss_in = move(loss1, image_partner)

    di0 = dot(w00, t0) + dot(w01, t1)
    dt0 = dot(w00.T, i0) + dot(w10.T, i1)
    gi0 = project(inv_i0, unit_i0, scale * di0)
    gt0 = project(inv_t0, unit_t0, scale * dt0)
    grad_image = (gi0 + gi.astype(jnp.float32)).astype(jnp.bfloat16)
    grad_text = (gt0 + gt.astype(jnp.float32)).astype(jnp.bfloat16)
    return (loss0 + loss_in, grad_image, grad_text)


def solution(mesh):
    in_specs = (P(("blk", "grp"), None), P(("blk", "grp"), None), P(), P())
    out_specs = (P(("blk", "grp")), P(("blk", "grp"), None), P(("blk", "grp"), None))
    return jax.shard_map(
        on_device, mesh=mesh, in_specs=in_specs, out_specs=out_specs, check_vma=False
    )
```

```python
import jax
import jax.numpy as jnp
from jax import lax
from jax.experimental import pallas as pl
from jax.experimental.pallas import tpu as pltpu
from jax.sharding import PartitionSpec as P

def paired(b, n):
    return b ^ 1


def crossed(b, n):
    return (b - 1 if b % 2 == 0 else b + 1) % n


def ring_out(b, n):
    return (b - 4 if b % 2 == 0 else b + 4) % n


def ring_back(b, n):
    return (b + 4 if b % 2 == 0 else b - 4) % n


def move(block, even, odd):
    n_blk, n_grp = lax.axis_size("blk"), lax.axis_size("grp")
    route = [
        (b * n_grp + g, (odd if g % 2 else even)(b, n_blk) * n_grp + g)
        for b in range(n_blk)
        for g in range(n_grp)
    ]
    return lax.ppermute(block, ("blk", "grp"), route)


def swap_image(block):
    return move(block, paired, crossed)


def swap_text(block):
    return move(block, crossed, paired)


def pass_text(block):
    return move(block, ring_out, ring_back)


def pass_image(block):
    return move(block, ring_back, ring_out)


def normalize(ref):
    wide = ref[...].astype(jnp.float32)
    inv = lax.rsqrt(jnp.sum(wide * wide, axis=-1, keepdims=True) + 1e-06)
    unit = wide * inv
    return inv, unit, unit.astype(jnp.bfloat16)


def project(inv, unit, grad):
    return inv * (grad - unit * jnp.sum(unit * grad, axis=-1, keepdims=True))


def dot_nt(a, b):
    return lax.dot_general(a, b, (((1,), (1,)), ((), ())), preferred_element_type=jnp.float32)


def dot_nn(a, b):
    return jnp.dot(a, b, preferred_element_type=jnp.float32)


def dot_tn(a, b):
    return lax.dot_general(a, b, (((0,), (0,)), ((), ())), preferred_element_type=jnp.float32)


def pair_of(scalars, img, txt, own=False):
    logits = scalars[0] * dot_nt(img, txt) + scalars[1]
    small = jnp.exp(-jnp.abs(logits))
    part = 1.0 / (1.0 + small)
    weights = jnp.where(logits >= 0, part, small * part)
    if own:
        hit = lax.broadcasted_iota(jnp.int32, logits.shape, 0) == lax.broadcasted_iota(
            jnp.int32, logits.shape, 1
        )
        weights = jnp.where(hit, weights - 1.0, weights)
        logits = jnp.where(hit, -logits, logits)
    losses = jnp.sum(jnp.maximum(logits, 0.0) + jnp.log1p(small), axis=-1, keepdims=True)
    return losses, weights.astype(jnp.bfloat16)


def main_kernel(scalars, i0_ref, t0_ref, i1_ref, t1_ref, gi0, gt0, di1, dt1, loss0, loss1):
    scale = scalars[0]
    inv_i0, unit_i0, i0 = normalize(i0_ref)
    inv_t0, unit_t0, t0 = normalize(t0_ref)
    _, _, i1 = normalize(i1_ref)
    _, _, t1 = normalize(t1_ref)
    a, w00 = pair_of(scalars, i0, t0, own=True)
    b, w01 = pair_of(scalars, i0, t1)
    loss0[...] = a + b
    a, w10 = pair_of(scalars, i1, t0)
    b, w11 = pair_of(scalars, i1, t1)
    loss1[...] = a + b
    di1[...] = dot_nn(w10, t0) + dot_nn(w11, t1)
    dt1[...] = dot_tn(w01, i0) + dot_tn(w11, i1)
    gi0[...] = project(inv_i0, unit_i0, scale * (dot_nn(w00, t0) + dot_nn(w01, t1)))
    gt0[...] = project(inv_t0, unit_t0, scale * (dot_tn(w00, i0) + dot_tn(w10, i1)))


def rest_kernel(scalars, i1_ref, t1_ref, ir_ref, tr_ref, di1, dt1, loss1, gi1, gt1, loss):
    scale = scalars[0]
    inv_i1, unit_i1, i1 = normalize(i1_ref)
    inv_t1, unit_t1, t1 = normalize(t1_ref)
    _, _, ir = normalize(ir_ref)
    _, _, tr = normalize(tr_ref)
    a, w1r = pair_of(scalars, i1, tr)
    loss[...] = loss1[...] + a
    _, wr1 = pair_of(scalars, ir, t1)
    gi1[...] = project(inv_i1, unit_i1, scale * (di1[...] + dot_nn(w1r, tr))).astype(jnp.bfloat16)
    gt1[...] = project(inv_t1, unit_t1, scale * (dt1[...] + dot_tn(wr1, ir))).astype(jnp.bfloat16)


def call(kernel, name, outs, flops, *args):
    vmem = pl.BlockSpec(memory_space=pltpu.VMEM)
    return pl.pallas_call(
        kernel,
        name=name,
        out_shape=outs,
        in_specs=[pl.BlockSpec(memory_space=pltpu.SMEM)] + [vmem] * (len(args) - 1),
        out_specs=[vmem] * len(outs),
        compiler_params=pltpu.CompilerParams(vmem_limit_bytes=40 * 1024 * 1024),
        cost_estimate=pl.CostEstimate(
            flops=flops, bytes_accessed=8 * 1024 * 1024, transcendentals=0
        ),
    )(*args)


def on_device(image_embed, text_embed, log_temp, logit_bias):
    rows, wide = image_embed.shape
    scalars = jnp.concatenate([jnp.exp(log_temp), logit_bias])
    full = jax.ShapeDtypeStruct((rows, wide), jnp.float32)
    half = jax.ShapeDtypeStruct((rows, wide), jnp.bfloat16)
    column = jax.ShapeDtypeStruct((rows, 1), jnp.float32)
    product = 2 * rows * rows * wide

    i1 = swap_image(image_embed)
    t1 = swap_text(text_embed)
    ir = pass_image(i1)
    tr = pass_text(t1)
    gi0, gt0, di1, dt1, loss0, loss1 = call(
        main_kernel, "main", [full] * 4 + [column] * 2, 12 * product,
        scalars, image_embed, text_embed, i1, t1,
    )
    gi1, gt1, loss1 = call(
        rest_kernel, "rest", [half, half, column], 4 * product,
        scalars, i1, t1, ir, tr, di1, dt1, loss1,
    )
    gi = swap_image(gi1)
    gt = swap_text(gt1)
    loss_in = swap_image(loss1.reshape(rows))
    grad_image = (gi0 + gi.astype(jnp.float32)).astype(jnp.bfloat16)
    grad_text = (gt0 + gt.astype(jnp.float32)).astype(jnp.bfloat16)
    return (loss0.reshape(rows) + loss_in, grad_image, grad_text)


def solution(mesh):
    in_specs = (P(("blk", "grp"), None), P(("blk", "grp"), None), P(), P())
    out_specs = (P(("blk", "grp")), P(("blk", "grp"), None), P(("blk", "grp"), None))
    return jax.shard_map(
        on_device, mesh=mesh, in_specs=in_specs, out_specs=out_specs, check_vma=False
    )
```

```python
import jax
import jax.numpy as jnp
from jax import lax
from jax.experimental import pallas as pl
from jax.experimental.pallas import tpu as pltpu
from jax.sharding import PartitionSpec as P

def paired(b, n):
    return b ^ 1


def crossed(b, n):
    return (b - 1 if b % 2 == 0 else b + 1) % n


def ring_out(b, n):
    return (b - 4 if b % 2 == 0 else b + 4) % n


def ring_back(b, n):
    return (b + 4 if b % 2 == 0 else b - 4) % n


def move(block, even, odd):
    n_blk, n_grp = lax.axis_size("blk"), lax.axis_size("grp")
    route = [
        (b * n_grp + g, (odd if g % 2 else even)(b, n_blk) * n_grp + g)
        for b in range(n_blk)
        for g in range(n_grp)
    ]
    return lax.ppermute(block, ("blk", "grp"), route)


def everywhere(block, target):
    return move(block, target, target)


def normalize(ref):
    wide = ref[...].astype(jnp.float32)
    inv = lax.rsqrt(jnp.sum(wide * wide, axis=-1, keepdims=True) + 1e-06)
    unit = wide * inv
    return inv, unit, unit.astype(jnp.bfloat16)


def project(inv, unit, grad):
    return inv * (grad - unit * jnp.sum(unit * grad, axis=-1, keepdims=True))


def dot_nt(a, b):
    return lax.dot_general(a, b, (((1,), (1,)), ((), ())), preferred_element_type=jnp.float32)


def dot_nn(a, b):
    return jnp.dot(a, b, preferred_element_type=jnp.float32)


def dot_tn(a, b):
    return lax.dot_general(a, b, (((0,), (0,)), ((), ())), preferred_element_type=jnp.float32)


def pair_of(scalars, img, txt, own=False):
    logits = scalars[0] * dot_nt(img, txt) + scalars[1]
    small = jnp.exp(-jnp.abs(logits))
    part = 1.0 / (1.0 + small)
    weights = jnp.where(logits >= 0, part, small * part)
    if own:
        hit = lax.broadcasted_iota(jnp.int32, logits.shape, 0) == lax.broadcasted_iota(
            jnp.int32, logits.shape, 1
        )
        weights = jnp.where(hit, weights - 1.0, weights)
        logits = jnp.where(hit, -logits, logits)
    losses = jnp.sum(jnp.maximum(logits, 0.0) + jnp.log1p(small), axis=-1, keepdims=True)
    return losses, weights.astype(jnp.bfloat16)


def own_kernel(scalars, i0_ref, t0_ref, i0_hat, t0_hat, w00, loss00):
    _, _, i0 = normalize(i0_ref)
    _, _, t0 = normalize(t0_ref)
    i0_hat[...] = i0
    t0_hat[...] = t0
    loss00[...], w00[...] = pair_of(scalars, i0, t0, own=True)


def main_kernel(
    scalars, i0_hat, t0_hat, i1_ref, t1_ref, loss00,
    i1_hat, t1_hat, inv_i, inv_t, w01, w10, di1, dt1, loss0, loss1,
):
    inv_i[...], _, i1 = normalize(i1_ref)
    inv_t[...], _, t1 = normalize(t1_ref)
    i1_hat[...] = i1
    t1_hat[...] = t1
    i0, t0 = i0_hat[...], t0_hat[...]
    a, w01_ = pair_of(scalars, i0, t1)
    loss0[...] = loss00[...] + a
    a, w10_ = pair_of(scalars, i1, t0)
    b, w11 = pair_of(scalars, i1, t1)
    loss1[...] = a + b
    w01[...] = w01_
    w10[...] = w10_
    di1[...] = dot_nn(w10_, t0) + dot_nn(w11, t1)
    dt1[...] = dot_tn(w01_, i0) + dot_tn(w11, i1)


def rest_kernel(
    scalars, i1_ref, t1_ref, i1_hat, t1_hat, inv_i, inv_t, ir_ref, tr_ref, di1, dt1, loss1,
    first, second, loss,
):
    scale, odd = scalars[0], scalars[2] > 0.5
    _, _, ir = normalize(ir_ref)
    _, _, tr = normalize(tr_ref)
    i1, t1 = i1_hat[...], t1_hat[...]
    a, w1r = pair_of(scalars, i1, tr)
    loss[...] = loss1[...] + a
    _, wr1 = pair_of(scalars, ir, t1)
    gi = project(
        inv_i[...], i1_ref[...].astype(jnp.float32) * inv_i[...],
        scale * (di1[...] + dot_nn(w1r, tr)),
    )
    gt = project(
        inv_t[...], t1_ref[...].astype(jnp.float32) * inv_t[...],
        scale * (dt1[...] + dot_tn(wr1, ir)),
    )
    first[...] = jnp.where(odd, gt, gi).astype(jnp.bfloat16)
    second[...] = jnp.where(odd, gi, gt).astype(jnp.bfloat16)


def home_kernel(
    scalars, i0_ref, t0_ref, i0_hat, t0_hat, i1_hat, t1_hat, w00, w01, w10, after, gi0, gt0
):
    scale = scalars[0]
    inv_i, unit_i, _ = normalize(i0_ref)
    inv_t, unit_t, _ = normalize(t0_ref)
    i0, t0, i1, t1 = i0_hat[...], t0_hat[...], i1_hat[...], t1_hat[...]
    gi0[...] = project(inv_i, unit_i, scale * (dot_nn(w00[...], t0) + dot_nn(w01[...], t1)))
    gt0[...] = project(inv_t, unit_t, scale * (dot_tn(w00[...], i0) + dot_tn(w10[...], i1)))


def sum_kernel(scalars, gi0, gt0, first, second, grad_image, grad_text):
    odd = scalars[2] > 0.5
    a, b = first[...].astype(jnp.float32), second[...].astype(jnp.float32)
    grad_image[...] = (gi0[...] + jnp.where(odd, b, a)).astype(jnp.bfloat16)
    grad_text[...] = (gt0[...] + jnp.where(odd, a, b)).astype(jnp.bfloat16)


def call(kernel, name, outs, flops, *args, steps=1):
    def spec(array):
        if steps == 1:
            return pl.BlockSpec(memory_space=pltpu.VMEM)
        return pl.BlockSpec((array.shape[0] // steps, array.shape[1]), lambda i: (i, 0))

    return pl.pallas_call(
        kernel,
        name=name,
        grid=(steps,) if steps > 1 else (),
        out_shape=outs,
        in_specs=[pl.BlockSpec(memory_space=pltpu.SMEM)] + [spec(a) for a in args[1:]],
        out_specs=[spec(a) for a in outs],
        compiler_params=pltpu.CompilerParams(vmem_limit_bytes=40 * 1024 * 1024),
        cost_estimate=pl.CostEstimate(
            flops=flops, bytes_accessed=8 * 1024 * 1024, transcendentals=0
        ),
    )(*args)


def on_device(image_embed, text_embed, log_temp, logit_bias):
    rows, wide = image_embed.shape
    odd = (lax.axis_index("grp") & 1).astype(jnp.float32)
    scalars = jnp.concatenate([jnp.exp(log_temp), logit_bias, odd[None]])
    full = jax.ShapeDtypeStruct((rows, wide), jnp.float32)
    half = jax.ShapeDtypeStruct((rows, wide), jnp.bfloat16)
    square = jax.ShapeDtypeStruct((rows, rows), jnp.bfloat16)
    column = jax.ShapeDtypeStruct((rows, 1), jnp.float32)
    product = 2 * rows * rows * wide

    i1 = everywhere(image_embed, paired)
    t1 = everywhere(text_embed, crossed)
    i0_hat, t0_hat, w00, loss00 = call(
        own_kernel, "own", [half, half, square, column], product,
        scalars, image_embed, text_embed,
    )
    i1, i0_hat = lax.optimization_barrier((i1, i0_hat))
    ir = everywhere(i1, ring_back)
    tr = everywhere(t1, ring_out)
    i1_hat, t1_hat, inv_i, inv_t, w01, w10, di1, dt1, loss0, loss1 = call(
        main_kernel, "main",
        [half, half, column, column, square, square, full, full, column, column], 7 * product,
        scalars, i0_hat, t0_hat, i1, t1, loss00,
    )
    first, second, loss1 = call(
        rest_kernel, "rest", [half, half, column], 4 * product,
        scalars, i1, t1, i1_hat, t1_hat, inv_i, inv_t, ir, tr, di1, dt1, loss1,
    )
    first = move(first, paired, crossed)
    second = move(second, crossed, paired)
    loss_in = everywhere(loss1.reshape(rows), paired)
    gi0, gt0 = call(
        home_kernel, "home", [full, full], 4 * product,
        scalars, image_embed, text_embed, i0_hat, t0_hat, i1_hat, t1_hat, w00, w01, w10, loss1,
    )
    grad_image, grad_text = call(
        sum_kernel, "total", [half, half], 4 * rows * wide,
        scalars, gi0, gt0, first, second, steps=4,
    )
    return (loss0.reshape(rows) + loss_in, grad_image, grad_text)


def solution(mesh):
    in_specs = (P(("blk", "grp"), None), P(("blk", "grp"), None), P(), P())
    out_specs = (P(("blk", "grp")), P(("blk", "grp"), None), P(("blk", "grp"), None))
    return jax.shard_map(
        on_device, mesh=mesh, in_specs=in_specs, out_specs=out_specs, check_vma=False
    )
```

```python
import jax
import jax.numpy as jnp
from jax import lax
from jax.experimental import pallas as pl
from jax.experimental.pallas import tpu as pltpu
from jax.sharding import PartitionSpec as P

def paired(b, n):
    return b ^ 1


def crossed(b, n):
    return (b - 1 if b % 2 == 0 else b + 1) % n


def ring_out(b, n):
    return (b - 4 if b % 2 == 0 else b + 4) % n


def ring_back(b, n):
    return (b + 4 if b % 2 == 0 else b - 4) % n


def move(block, even, odd):
    n_blk, n_grp = lax.axis_size("blk"), lax.axis_size("grp")
    route = [
        (b * n_grp + g, (odd if g % 2 else even)(b, n_blk) * n_grp + g)
        for b in range(n_blk)
        for g in range(n_grp)
    ]
    return lax.ppermute(block, ("blk", "grp"), route)


def swap_image(block):
    return move(block, paired, crossed)


def swap_text(block):
    return move(block, crossed, paired)


def pass_text(block):
    return move(block, ring_out, ring_back)


def pass_image(block):
    return move(block, ring_back, ring_out)


def normalize(ref):
    wide = ref[...].astype(jnp.float32)
    inv = lax.rsqrt(jnp.sum(wide * wide, axis=-1, keepdims=True) + 1e-06)
    unit = wide * inv
    return inv, unit, unit.astype(jnp.bfloat16)


def project(inv, unit, grad):
    return inv * (grad - unit * jnp.sum(unit * grad, axis=-1, keepdims=True))


def dot_nt(a, b):
    return lax.dot_general(a, b, (((1,), (1,)), ((), ())), preferred_element_type=jnp.float32)


def dot_nn(a, b):
    return jnp.dot(a, b, preferred_element_type=jnp.float32)


def dot_tn(a, b):
    return lax.dot_general(a, b, (((0,), (0,)), ((), ())), preferred_element_type=jnp.float32)


def pair_of(scalars, img, txt, own=False):
    logits = scalars[0] * dot_nt(img, txt) + scalars[1]
    small = jnp.exp(-jnp.abs(logits))
    part = 1.0 / (1.0 + small)
    weights = jnp.where(logits >= 0, part, small * part)
    if own:
        hit = lax.broadcasted_iota(jnp.int32, logits.shape, 0) == lax.broadcasted_iota(
            jnp.int32, logits.shape, 1
        )
        weights = jnp.where(hit, weights - 1.0, weights)
        logits = jnp.where(hit, -logits, logits)
    losses = jnp.sum(jnp.maximum(logits, 0.0) + jnp.log1p(small), axis=-1, keepdims=True)
    return losses, weights.astype(jnp.bfloat16)


def own_kernel(i0_ref, t0_ref, i0_hat, t0_hat):
    _, _, i0_hat[...] = normalize(i0_ref)
    _, _, t0_hat[...] = normalize(t0_ref)


def main_kernel(
    scalars, i0_hat, t0_hat, i1_ref, t1_ref, i1_hat, t1_hat, inv_i, inv_t, di1, dt1, loss1
):
    inv_i[...], _, i1 = normalize(i1_ref)
    inv_t[...], _, t1 = normalize(t1_ref)
    i1_hat[...] = i1
    t1_hat[...] = t1
    i0, t0 = i0_hat[...], t0_hat[...]
    _, w01 = pair_of(scalars, i0, t1)
    a, w11 = pair_of(scalars, i1, t1)
    dt1[...] = dot_tn(w01, i0) + dot_tn(w11, i1)
    b, w10 = pair_of(scalars, i1, t0)
    loss1[...] = a + b
    di1[...] = dot_nn(w10, t0) + dot_nn(w11, t1)


def text_kernel(scalars, t1_ref, t1_hat, inv_t, ir_ref, dt1, gt1):
    _, _, ir = normalize(ir_ref)
    _, weights = pair_of(scalars, ir, t1_hat[...])
    unit = t1_ref[...].astype(jnp.float32) * inv_t[...]
    grad = scalars[0] * (dt1[...] + dot_tn(weights, ir))
    gt1[...] = project(inv_t[...], unit, grad).astype(jnp.bfloat16)


def image_kernel(scalars, i1_ref, i1_hat, inv_i, tr_ref, di1, loss1, gi1, loss):
    _, _, tr = normalize(tr_ref)
    losses, weights = pair_of(scalars, i1_hat[...], tr)
    loss[...] = loss1[...] + losses
    unit = i1_ref[...].astype(jnp.float32) * inv_i[...]
    grad = scalars[0] * (di1[...] + dot_nn(weights, tr))
    gi1[...] = project(inv_i[...], unit, grad).astype(jnp.bfloat16)


def home_kernel(scalars, i0_ref, t0_ref, i1_hat, t1_hat, after, gi0, gt0, loss0):
    scale = scalars[0]
    inv_i, unit_i, i0 = normalize(i0_ref)
    inv_t, unit_t, t0 = normalize(t0_ref)
    i1, t1 = i1_hat[...], t1_hat[...]
    a, w00 = pair_of(scalars, i0, t0, own=True)
    b, w01 = pair_of(scalars, i0, t1)
    loss0[...] = a + b
    _, w10 = pair_of(scalars, i1, t0)
    gi0[...] = project(inv_i, unit_i, scale * (dot_nn(w00, t0) + dot_nn(w01, t1)))
    gt0[...] = project(inv_t, unit_t, scale * (dot_tn(w00, i0) + dot_tn(w10, i1)))


def sum_kernel(gi0, gt0, gi, gt, grad_image, grad_text):
    grad_image[...] = (gi0[...] + gi[...].astype(jnp.float32)).astype(jnp.bfloat16)
    grad_text[...] = (gt0[...] + gt[...].astype(jnp.float32)).astype(jnp.bfloat16)


def call(kernel, name, outs, flops, *args, steps=1):
    def spec(array):
        if array.ndim == 1:
            return pl.BlockSpec(memory_space=pltpu.SMEM)
        if steps == 1:
            return pl.BlockSpec(memory_space=pltpu.VMEM)
        return pl.BlockSpec((array.shape[0] // steps, array.shape[1]), lambda i: (i, 0))

    return pl.pallas_call(
        kernel,
        name=name,
        grid=(steps,) if steps > 1 else (),
        out_shape=outs,
        in_specs=[spec(a) for a in args],
        out_specs=[spec(a) for a in outs],
        compiler_params=pltpu.CompilerParams(vmem_limit_bytes=40 * 1024 * 1024),
        cost_estimate=pl.CostEstimate(
            flops=flops, bytes_accessed=4 * 1024 * 1024, transcendentals=0
        ),
    )(*args)


def on_device(image_embed, text_embed, log_temp, logit_bias):
    rows, wide = image_embed.shape
    scalars = jnp.concatenate([jnp.exp(log_temp), logit_bias])
    full = jax.ShapeDtypeStruct((rows, wide), jnp.float32)
    half = jax.ShapeDtypeStruct((rows, wide), jnp.bfloat16)
    column = jax.ShapeDtypeStruct((rows, 1), jnp.float32)
    product = 2 * rows * rows * wide

    i1 = swap_image(image_embed)
    t1 = swap_text(text_embed)
    i0_hat, t0_hat = call(own_kernel, "own", [half, half], product, image_embed, text_embed)
    i1, i0_hat, scalars = lax.optimization_barrier((i1, i0_hat, scalars))
    ir = pass_image(i1)
    tr = pass_text(t1)
    i1_hat, t1_hat, inv_i, inv_t, di1, dt1, loss1 = call(
        main_kernel, "main", [half, half, column, column, full, full, column], 7 * product,
        scalars, i0_hat, t0_hat, i1, t1,
    )
    (gt1,) = call(
        text_kernel, "text_share", [half], 2 * product,
        scalars, t1, t1_hat, inv_t, ir, dt1,
    )
    gt = swap_text(gt1)
    gi1, loss1 = call(
        image_kernel, "image_share", [half, column], 2 * product,
        scalars, i1, i1_hat, inv_i, tr, di1, loss1,
    )
    gi = swap_image(gi1)
    loss_in = swap_image(loss1.reshape(rows))
    gi0, gt0, loss0 = call(
        home_kernel, "home", [full, full, column], 7 * product,
        scalars, image_embed, text_embed, i1_hat, t1_hat, loss1,
    )
    grad_image, grad_text = call(
        sum_kernel, "total", [half, half], 4 * rows * wide, gi0, gt0, gi, gt, steps=4
    )
    return (loss0.reshape(rows) + loss_in, grad_image, grad_text)


def solution(mesh):
    in_specs = (P(("blk", "grp"), None), P(("blk", "grp"), None), P(), P())
    out_specs = (P(("blk", "grp")), P(("blk", "grp"), None), P(("blk", "grp"), None))
    return jax.shard_map(
        on_device, mesh=mesh, in_specs=in_specs, out_specs=out_specs, check_vma=False
    )
```

```python
import jax
import jax.numpy as jnp
from jax import lax
from jax.experimental import pallas as pl
from jax.experimental.pallas import tpu as pltpu
from jax.sharding import PartitionSpec as P

EXTRA = 8
PIECES = 3


def paired(b, n):
    return b ^ 1


def crossed(b, n):
    return (b - 1 if b % 2 == 0 else b + 1) % n


def ring_out(b, n):
    return (b - 4 if b % 2 == 0 else b + 4) % n


def ring_back(b, n):
    return (b + 4 if b % 2 == 0 else b - 4) % n


def move(block, even, odd):
    n_blk, n_grp = lax.axis_size("blk"), lax.axis_size("grp")
    route = [
        (b * n_grp + g, (odd if (g + (g + 2) // 4) % 2 else even)(b, n_blk) * n_grp + g)
        for b in range(n_blk)
        for g in range(n_grp)
    ]
    return lax.ppermute(block, ("blk", "grp"), route)


def swap_image(block):
    return move(block, paired, crossed)


def swap_text(block):
    return move(block, crossed, paired)


def pass_text(block):
    return move(block, ring_out, ring_back)


def pass_image(block):
    return move(block, ring_back, ring_out)


def normalize(ref):
    wide = ref[...].astype(jnp.float32)
    inv = lax.rsqrt(jnp.sum(wide * wide, axis=-1, keepdims=True) + 1e-06)
    unit = wide * inv
    return inv, unit, unit.astype(jnp.bfloat16)


def project(inv, unit, grad):
    return inv * (grad - unit * jnp.sum(unit * grad, axis=-1, keepdims=True))


def dot_nt(a, b):
    return lax.dot_general(a, b, (((1,), (1,)), ((), ())), preferred_element_type=jnp.float32)


def dot_nn(a, b):
    return jnp.dot(a, b, preferred_element_type=jnp.float32)


def dot_tn(a, b):
    return lax.dot_general(a, b, (((0,), (0,)), ((), ())), preferred_element_type=jnp.float32)


def pair_of(scalars, img, txt, own=False):
    logits = scalars[0] * dot_nt(img, txt) + scalars[1]
    small = jnp.exp(-jnp.abs(logits))
    part = 1.0 / (1.0 + small)
    weights = jnp.where(logits >= 0, part, small * part)
    if own:
        hit = lax.broadcasted_iota(jnp.int32, logits.shape, 0) == lax.broadcasted_iota(
            jnp.int32, logits.shape, 1
        )
        weights = jnp.where(hit, weights - 1.0, weights)
        logits = jnp.where(hit, -logits, logits)
    losses = jnp.sum(jnp.maximum(logits, 0.0) + jnp.log1p(small), axis=-1, keepdims=True)
    return losses, weights.astype(jnp.bfloat16)


def own_kernel(i0_ref, t0_ref, i0_hat, t0_hat):
    _, _, i0_hat[...] = normalize(i0_ref)
    _, _, t0_hat[...] = normalize(t0_ref)


def main_kernel(
    scalars, i0_hat, t0_hat, i1_ref, t1_ref, i1_hat, t1_hat, inv_i, inv_t, di1, dt1, loss1
):
    inv_i[...], _, i1 = normalize(i1_ref)
    inv_t[...], _, t1 = normalize(t1_ref)
    i1_hat[...] = i1
    t1_hat[...] = t1
    i0, t0 = i0_hat[...], t0_hat[...]
    _, w01 = pair_of(scalars, i0, t1)
    a, w11 = pair_of(scalars, i1, t1)
    dt1[...] = dot_tn(w01, i0) + dot_tn(w11, i1)
    b, w10 = pair_of(scalars, i1, t0)
    loss1[...] = a + b
    di1[...] = dot_nn(w10, t0) + dot_nn(w11, t1)


def text_kernel(scalars, t1_ref, t1_hat, inv_t, ir_ref, dt1, gt1):
    _, _, ir = normalize(ir_ref)
    _, weights = pair_of(scalars, ir, t1_hat[...])
    unit = t1_ref[...].astype(jnp.float32) * inv_t[...]
    grad = scalars[0] * (dt1[...] + dot_tn(weights, ir))
    gt1[...] = project(inv_t[...], unit, grad).astype(jnp.bfloat16)


def image_kernel(scalars, i1_ref, i1_hat, inv_i, tr_ref, di1, loss1, gi1):
    rows = i1_ref.shape[0]
    _, _, tr = normalize(tr_ref)
    losses, weights = pair_of(scalars, i1_hat[...], tr)
    rest, lane = loss1[...] + losses, lax.broadcasted_iota(jnp.int32, (rows, 128), 1)
    packed = jnp.zeros((rows, 128), jnp.float32)
    for k in range(PIECES):
        piece = rest.astype(jnp.bfloat16).astype(jnp.float32)
        packed = jnp.where(lane == k, piece, packed)
        rest = rest - piece
    hit = lax.broadcasted_iota(jnp.int32, (rows, rows), 0) == lax.broadcasted_iota(
        jnp.int32, (rows, rows), 1
    )
    lines = dot_tn(packed.astype(jnp.bfloat16), hit.astype(jnp.bfloat16))
    gi1[rows:, :] = jnp.zeros((EXTRA, gi1.shape[1]), jnp.bfloat16)
    gi1[rows:, :rows] = lines[:EXTRA].astype(jnp.bfloat16)
    unit = i1_ref[...].astype(jnp.float32) * inv_i[...]
    grad = scalars[0] * (di1[...] + dot_nn(weights, tr))
    gi1[:rows, :] = project(inv_i[...], unit, grad).astype(jnp.bfloat16)


def home_kernel(scalars, i0_ref, t0_ref, i1_hat, t1_hat, gi0, gt0, loss0):
    scale = scalars[0]
    inv_i, unit_i, i0 = normalize(i0_ref)
    inv_t, unit_t, t0 = normalize(t0_ref)
    i1, t1 = i1_hat[...], t1_hat[...]
    a, w00 = pair_of(scalars, i0, t0, own=True)
    b, w01 = pair_of(scalars, i0, t1)
    loss0[...] = a + b
    _, w10 = pair_of(scalars, i1, t0)
    gi0[...] = project(inv_i, unit_i, scale * (dot_nn(w00, t0) + dot_nn(w01, t1)))
    gt0[...] = project(inv_t, unit_t, scale * (dot_tn(w00, i0) + dot_tn(w10, i1)))


def sum_kernel(gi0, gt0, gi, gt, grad_image, grad_text):
    grad_image[...] = (gi0[...] + gi[...].astype(jnp.float32)).astype(jnp.bfloat16)
    grad_text[...] = (gt0[...] + gt[...].astype(jnp.float32)).astype(jnp.bfloat16)


def call(kernel, name, outs, flops, *args, steps=1):
    def spec(array):
        if array.ndim == 1:
            return pl.BlockSpec(memory_space=pltpu.SMEM)
        if steps == 1:
            return pl.BlockSpec(memory_space=pltpu.VMEM)
        return pl.BlockSpec((outs[0].shape[0] // steps, array.shape[1]), lambda i: (i, 0))

    return pl.pallas_call(
        kernel,
        name=name,
        grid=(steps,) if steps > 1 else (),
        out_shape=outs,
        in_specs=[spec(a) for a in args],
        out_specs=[spec(a) for a in outs],
        compiler_params=pltpu.CompilerParams(vmem_limit_bytes=40 * 1024 * 1024),
        cost_estimate=pl.CostEstimate(
            flops=flops, bytes_accessed=4 * 1024 * 1024, transcendentals=0
        ),
    )(*args)


def on_device(image_embed, text_embed, log_temp, logit_bias):
    rows, wide = image_embed.shape
    scalars = jnp.concatenate([jnp.exp(log_temp), logit_bias])
    full = jax.ShapeDtypeStruct((rows, wide), jnp.float32)
    half = jax.ShapeDtypeStruct((rows, wide), jnp.bfloat16)
    column = jax.ShapeDtypeStruct((rows, 1), jnp.float32)
    product = 2 * rows * rows * wide

    i1 = swap_image(image_embed)
    t1 = swap_text(text_embed)
    i0_hat, t0_hat = call(own_kernel, "own", [half, half], product, image_embed, text_embed)
    t1, i0_hat, scalars = lax.optimization_barrier((t1, i0_hat, scalars))
    ir = pass_image(i1)
    tr = pass_text(t1)
    i1_hat, t1_hat, inv_i, inv_t, di1, dt1, loss1 = call(
        main_kernel, "main", [half, half, column, column, full, full, column], 7 * product,
        scalars, i0_hat, t0_hat, i1, t1,
    )
    (gt1,) = call(
        text_kernel, "text_share", [half], 2 * product,
        scalars, t1, t1_hat, inv_t, ir, dt1,
    )
    gt = swap_text(gt1)
    taller = jax.ShapeDtypeStruct((rows + EXTRA, wide), jnp.bfloat16)
    (gi1,) = call(
        image_kernel, "image_share", [taller], 2 * product,
        scalars, i1, i1_hat, inv_i, tr, di1, loss1,
    )
    gi = swap_image(gi1)
    i1_hat, gi1 = lax.optimization_barrier((i1_hat, gi1))
    gi0, gt0, loss0 = call(
        home_kernel, "home", [full, full, column], 7 * product,
        scalars, image_embed, text_embed, i1_hat, t1_hat,
    )
    grad_image, grad_text = call(
        sum_kernel, "total", [half, half], 4 * rows * wide, gi0, gt0, gi, gt, steps=4
    )
    lines = gi[rows : rows + PIECES, :rows].astype(jnp.float32)
    return (loss0.reshape(rows) + jnp.sum(lines, axis=0), grad_image, grad_text)


def solution(mesh):
    in_specs = (P(("blk", "grp"), None), P(("blk", "grp"), None), P(), P())
    out_specs = (P(("blk", "grp")), P(("blk", "grp"), None), P(("blk", "grp"), None))
    return jax.shard_map(
        on_device, mesh=mesh, in_specs=in_specs, out_specs=out_specs, check_vma=False
    )
```

```python
import jax
import jax.numpy as jnp
from jax import lax
from jax.experimental import pallas as pl
from jax.experimental.pallas import tpu as pltpu
from jax.sharding import PartitionSpec as P

EXTRA = 8
PIECES = 3


def paired(b, n):
    return b ^ 1


def crossed(b, n):
    return (b - 1 if b % 2 == 0 else b + 1) % n


def ring_out(b, n):
    return (b - 4 if b % 2 == 0 else b + 4) % n


def ring_back(b, n):
    return (b + 4 if b % 2 == 0 else b - 4) % n


def move(block, even, odd):
    n_blk, n_grp = lax.axis_size("blk"), lax.axis_size("grp")
    route = [
        (b * n_grp + g, (odd if (g + (g + 2) // 4) % 2 else even)(b, n_blk) * n_grp + g)
        for b in range(n_blk)
        for g in range(n_grp)
    ]
    return lax.ppermute(block, ("blk", "grp"), route)


def swap_image(block):
    return move(block, paired, crossed)


def swap_text(block):
    return move(block, crossed, paired)


def pass_text(block):
    return move(block, ring_out, ring_back)


def pass_image(block):
    return move(block, ring_back, ring_out)


def normalize(ref):
    wide = ref[...].astype(jnp.float32)
    inv = lax.rsqrt(jnp.sum(wide * wide, axis=-1, keepdims=True) + 1e-06)
    unit = wide * inv
    return inv, unit, unit.astype(jnp.bfloat16)


def project(inv, unit, grad):
    return inv * (grad - unit * jnp.sum(unit * grad, axis=-1, keepdims=True))


def dot_nt(a, b):
    return lax.dot_general(a, b, (((1,), (1,)), ((), ())), preferred_element_type=jnp.float32)


def dot_nn(a, b):
    return jnp.dot(a, b, preferred_element_type=jnp.float32)


def dot_tn(a, b):
    return lax.dot_general(a, b, (((0,), (0,)), ((), ())), preferred_element_type=jnp.float32)


def pair_of(scalars, img, txt, own=False):
    logits = scalars[0] * dot_nt(img, txt) + scalars[1]
    small = jnp.exp(-jnp.abs(logits))
    part = 1.0 / (1.0 + small)
    weights = jnp.where(logits >= 0, part, small * part)
    if own:
        hit = lax.broadcasted_iota(jnp.int32, logits.shape, 0) == lax.broadcasted_iota(
            jnp.int32, logits.shape, 1
        )
        weights = jnp.where(hit, weights - 1.0, weights)
        logits = jnp.where(hit, -logits, logits)
    losses = jnp.sum(jnp.maximum(logits, 0.0) + jnp.log1p(small), axis=-1, keepdims=True)
    return losses, weights.astype(jnp.bfloat16)


def own_kernel(i0_ref, t0_ref, i0_hat, t0_hat):
    _, _, i0_hat[...] = normalize(i0_ref)
    _, _, t0_hat[...] = normalize(t0_ref)


def main_kernel(
    scalars, i0_hat, t0_hat, i1_ref, t1_ref, i1_hat, t1_hat, inv_i, inv_t, di1, dt1, loss1
):
    inv_i[...], _, i1 = normalize(i1_ref)
    inv_t[...], _, t1 = normalize(t1_ref)
    i1_hat[...] = i1
    t1_hat[...] = t1
    i0, t0 = i0_hat[...], t0_hat[...]
    _, w01 = pair_of(scalars, i0, t1)
    a, w11 = pair_of(scalars, i1, t1)
    dt1[...] = dot_tn(w01, i0) + dot_tn(w11, i1)
    b, w10 = pair_of(scalars, i1, t0)
    loss1[...] = a + b
    di1[...] = dot_nn(w10, t0) + dot_nn(w11, t1)


def text_kernel(scalars, t1_ref, t1_hat, inv_t, ir_ref, dt1, gt1):
    _, _, ir = normalize(ir_ref)
    _, weights = pair_of(scalars, ir, t1_hat[...])
    unit = t1_ref[...].astype(jnp.float32) * inv_t[...]
    grad = scalars[0] * (dt1[...] + dot_tn(weights, ir))
    gt1[...] = project(inv_t[...], unit, grad).astype(jnp.bfloat16)


def image_kernel(scalars, i1_ref, i1_hat, inv_i, tr_ref, di1, loss1, gi1):
    rows = i1_ref.shape[0]
    _, _, tr = normalize(tr_ref)
    losses, weights = pair_of(scalars, i1_hat[...], tr)
    rest, lane = loss1[...] + losses, lax.broadcasted_iota(jnp.int32, (rows, 128), 1)
    packed = jnp.zeros((rows, 128), jnp.float32)
    for k in range(PIECES):
        piece = rest.astype(jnp.bfloat16).astype(jnp.float32)
        packed = jnp.where(lane == k, piece, packed)
        rest = rest - piece
    hit = lax.broadcasted_iota(jnp.int32, (rows, rows), 0) == lax.broadcasted_iota(
        jnp.int32, (rows, rows), 1
    )
    lines = dot_tn(packed.astype(jnp.bfloat16), hit.astype(jnp.bfloat16))
    gi1[rows:, :] = jnp.zeros((EXTRA, gi1.shape[1]), jnp.bfloat16)
    gi1[rows:, :rows] = lines[:EXTRA].astype(jnp.bfloat16)
    unit = i1_ref[...].astype(jnp.float32) * inv_i[...]
    grad = scalars[0] * (di1[...] + dot_nn(weights, tr))
    gi1[:rows, :] = project(inv_i[...], unit, grad).astype(jnp.bfloat16)


def home_kernel(scalars, i0_ref, t0_ref, i1_hat, t1_hat, gi0, gt0, loss0):
    scale = scalars[0]
    inv_i, unit_i, i0 = normalize(i0_ref)
    inv_t, unit_t, t0 = normalize(t0_ref)
    i1, t1 = i1_hat[...], t1_hat[...]
    a, w00 = pair_of(scalars, i0, t0, own=True)
    b, w01 = pair_of(scalars, i0, t1)
    loss0[...] = a + b
    _, w10 = pair_of(scalars, i1, t0)
    gi0[...] = project(inv_i, unit_i, scale * (dot_nn(w00, t0) + dot_nn(w01, t1)))
    gt0[...] = project(inv_t, unit_t, scale * (dot_tn(w00, i0) + dot_tn(w10, i1)))


def sum_kernel(gi0, gt0, gi, gt, grad_image, grad_text):
    grad_image[...] = (gi0[...] + gi[: gi0.shape[0], :].astype(jnp.float32)).astype(jnp.bfloat16)
    grad_text[...] = (gt0[...] + gt[...].astype(jnp.float32)).astype(jnp.bfloat16)


def call(kernel, name, outs, flops, *args):
    def spec(array):
        return pl.BlockSpec(memory_space=pltpu.SMEM if array.ndim == 1 else pltpu.VMEM)

    return pl.pallas_call(
        kernel,
        name=name,
        out_shape=outs,
        in_specs=[spec(a) for a in args],
        out_specs=[spec(a) for a in outs],
        compiler_params=pltpu.CompilerParams(vmem_limit_bytes=40 * 1024 * 1024),
        cost_estimate=pl.CostEstimate(
            flops=flops, bytes_accessed=4 * 1024 * 1024, transcendentals=0
        ),
    )(*args)


def on_device(image_embed, text_embed, log_temp, logit_bias):
    rows, wide = image_embed.shape
    scalars = jnp.concatenate([jnp.exp(log_temp), logit_bias])
    full = jax.ShapeDtypeStruct((rows, wide), jnp.float32)
    half = jax.ShapeDtypeStruct((rows, wide), jnp.bfloat16)
    column = jax.ShapeDtypeStruct((rows, 1), jnp.float32)
    product = 2 * rows * rows * wide

    i1 = swap_image(image_embed)
    t1 = swap_text(text_embed)
    i0_hat, t0_hat = call(own_kernel, "own", [half, half], product, image_embed, text_embed)
    t1, i0_hat, scalars = lax.optimization_barrier((t1, i0_hat, scalars))
    ir = pass_image(i1)
    tr = pass_text(t1)
    i1_hat, t1_hat, inv_i, inv_t, di1, dt1, loss1 = call(
        main_kernel, "main", [half, half, column, column, full, full, column], 7 * product,
        scalars, i0_hat, t0_hat, i1, t1,
    )
    (gt1,) = call(
        text_kernel, "text_share", [half], 2 * product,
        scalars, t1, t1_hat, inv_t, ir, dt1,
    )
    gt = swap_text(gt1)
    taller = jax.ShapeDtypeStruct((rows + EXTRA, wide), jnp.bfloat16)
    (gi1,) = call(
        image_kernel, "image_share", [taller], 2 * product,
        scalars, i1, i1_hat, inv_i, tr, di1, loss1,
    )
    gi = swap_image(gi1)
    i1_hat, gi1 = lax.optimization_barrier((i1_hat, gi1))
    gi0, gt0, loss0 = call(
        home_kernel, "home", [full, full, column], 7 * product,
        scalars, image_embed, text_embed, i1_hat, t1_hat,
    )
    grad_image, grad_text = call(
        sum_kernel, "total", [half, half], 4 * rows * wide, gi0, gt0, gi, gt
    )
    lines = gi[rows : rows + PIECES, :rows].astype(jnp.float32)
    return (loss0.reshape(rows) + jnp.sum(lines, axis=0), grad_image, grad_text)


def solution(mesh):
    in_specs = (P(("blk", "grp"), None), P(("blk", "grp"), None), P(), P())
    out_specs = (P(("blk", "grp")), P(("blk", "grp"), None), P(("blk", "grp"), None))
    return jax.shard_map(
        on_device, mesh=mesh, in_specs=in_specs, out_specs=out_specs, check_vma=False
    )
```

```python
import jax
import jax.numpy as jnp
from jax import lax
from jax.experimental import pallas as pl
from jax.experimental.pallas import tpu as pltpu
from jax.sharding import PartitionSpec as P

EXTRA = 8
PIECES = 3


def paired(b, n):
    return b ^ 1


def crossed(b, n):
    return (b - 1 if b % 2 == 0 else b + 1) % n


def ring_out(b, n):
    return (b - 4 if b % 2 == 0 else b + 4) % n


def ring_back(b, n):
    return (b + 4 if b % 2 == 0 else b - 4) % n


def move(block, even, odd):
    n_blk, n_grp = lax.axis_size("blk"), lax.axis_size("grp")
    route = [
        (b * n_grp + g, (odd if (g + (g + 2) // 4) % 2 else even)(b, n_blk) * n_grp + g)
        for b in range(n_blk)
        for g in range(n_grp)
    ]
    return lax.ppermute(block, ("blk", "grp"), route)


def swap_image(block):
    return move(block, paired, crossed)


def swap_text(block):
    return move(block, crossed, paired)


def pass_text(block):
    return move(block, ring_out, ring_back)


def pass_image(block):
    return move(block, ring_back, ring_out)


def normalize(ref):
    wide = ref[...].astype(jnp.float32)
    inv = lax.rsqrt(jnp.sum(wide * wide, axis=-1, keepdims=True) + 1e-06)
    unit = wide * inv
    return inv, unit, unit.astype(jnp.bfloat16)


def project(inv, unit, grad):
    return inv * (grad - unit * jnp.sum(unit * grad, axis=-1, keepdims=True))


def dot_nt(a, b):
    return lax.dot_general(a, b, (((1,), (1,)), ((), ())), preferred_element_type=jnp.float32)


def dot_nn(a, b):
    return jnp.dot(a, b, preferred_element_type=jnp.float32)


def dot_tn(a, b):
    return lax.dot_general(a, b, (((0,), (0,)), ((), ())), preferred_element_type=jnp.float32)


def pair_of(scalars, img, txt, own=False):
    logits = scalars[0] * dot_nt(img, txt) + scalars[1]
    small = jnp.exp(-jnp.abs(logits))
    part = 1.0 / (1.0 + small)
    weights = jnp.where(logits >= 0, part, small * part)
    if own:
        hit = lax.broadcasted_iota(jnp.int32, logits.shape, 0) == lax.broadcasted_iota(
            jnp.int32, logits.shape, 1
        )
        weights = jnp.where(hit, weights - 1.0, weights)
        logits = jnp.where(hit, -logits, logits)
    losses = jnp.sum(jnp.maximum(logits, 0.0) + jnp.log1p(small), axis=-1, keepdims=True)
    return losses, weights.astype(jnp.bfloat16)


def own_kernel(i0_ref, t0_ref, i0_hat, t0_hat):
    _, _, i0_hat[...] = normalize(i0_ref)
    _, _, t0_hat[...] = normalize(t0_ref)


def main_kernel(
    scalars, t0_hat, i1_ref, t1_ref, i1_hat, t1_hat, inv_i, inv_t, w11_ref, di1, loss1
):
    inv_i[...], _, i1 = normalize(i1_ref)
    inv_t[...], _, t1 = normalize(t1_ref)
    i1_hat[...] = i1
    t1_hat[...] = t1
    t0 = t0_hat[...]
    a, w11 = pair_of(scalars, i1, t1)
    w11_ref[...] = w11
    b, w10 = pair_of(scalars, i1, t0)
    loss1[...] = a + b
    di1[...] = dot_nn(w10, t0) + dot_nn(w11, t1)


def text_kernel(scalars, t1_ref, t1_hat, inv_t, ir_ref, i0_hat, i1_hat, w11, gt1):
    _, _, ir = normalize(ir_ref)
    i0, t1 = i0_hat[...], t1_hat[...]
    _, weights = pair_of(scalars, ir, t1)
    _, w01 = pair_of(scalars, i0, t1)
    total = dot_tn(w01, i0) + dot_tn(w11[...], i1_hat[...]) + dot_tn(weights, ir)
    unit = t1_ref[...].astype(jnp.float32) * inv_t[...]
    grad = scalars[0] * total
    gt1[...] = project(inv_t[...], unit, grad).astype(jnp.bfloat16)


def image_kernel(scalars, i1_ref, i1_hat, inv_i, tr_ref, di1, loss1, gi1):
    rows = i1_ref.shape[0]
    _, _, tr = normalize(tr_ref)
    losses, weights = pair_of(scalars, i1_hat[...], tr)
    rest, lane = loss1[...] + losses, lax.broadcasted_iota(jnp.int32, (rows, 128), 1)
    packed = jnp.zeros((rows, 128), jnp.float32)
    for k in range(PIECES):
        piece = rest.astype(jnp.bfloat16).astype(jnp.float32)
        packed = jnp.where(lane == k, piece, packed)
        rest = rest - piece
    hit = lax.broadcasted_iota(jnp.int32, (rows, rows), 0) == lax.broadcasted_iota(
        jnp.int32, (rows, rows), 1
    )
    lines = dot_tn(packed.astype(jnp.bfloat16), hit.astype(jnp.bfloat16))
    gi1[rows:, :] = jnp.zeros((EXTRA, gi1.shape[1]), jnp.bfloat16)
    gi1[rows:, :rows] = lines[:EXTRA].astype(jnp.bfloat16)
    unit = i1_ref[...].astype(jnp.float32) * inv_i[...]
    grad = scalars[0] * (di1[...] + dot_nn(weights, tr))
    gi1[:rows, :] = project(inv_i[...], unit, grad).astype(jnp.bfloat16)


def home_kernel(scalars, i0_ref, t0_ref, i1_hat, t1_hat, gi0, gt0, loss0):
    scale = scalars[0]
    inv_i, unit_i, i0 = normalize(i0_ref)
    inv_t, unit_t, t0 = normalize(t0_ref)
    i1, t1 = i1_hat[...], t1_hat[...]
    a, w00 = pair_of(scalars, i0, t0, own=True)
    b, w01 = pair_of(scalars, i0, t1)
    loss0[...] = a + b
    _, w10 = pair_of(scalars, i1, t0)
    gi0[...] = project(inv_i, unit_i, scale * (dot_nn(w00, t0) + dot_nn(w01, t1)))
    gt0[...] = project(inv_t, unit_t, scale * (dot_tn(w00, i0) + dot_tn(w10, i1)))


def sum_kernel(gi0, gt0, gi, gt, grad_image, grad_text):
    grad_image[...] = (gi0[...] + gi[: gi0.shape[0], :].astype(jnp.float32)).astype(jnp.bfloat16)
    grad_text[...] = (gt0[...] + gt[...].astype(jnp.float32)).astype(jnp.bfloat16)


def call(kernel, name, outs, flops, *args):
    def spec(array):
        return pl.BlockSpec(memory_space=pltpu.SMEM if array.ndim == 1 else pltpu.VMEM)

    return pl.pallas_call(
        kernel,
        name=name,
        out_shape=outs,
        in_specs=[spec(a) for a in args],
        out_specs=[spec(a) for a in outs],
        compiler_params=pltpu.CompilerParams(vmem_limit_bytes=40 * 1024 * 1024),
        cost_estimate=pl.CostEstimate(
            flops=flops, bytes_accessed=4 * 1024 * 1024, transcendentals=0
        ),
    )(*args)


def on_device(image_embed, text_embed, log_temp, logit_bias):
    rows, wide = image_embed.shape
    scalars = jnp.concatenate([jnp.exp(log_temp), logit_bias])
    full = jax.ShapeDtypeStruct((rows, wide), jnp.float32)
    half = jax.ShapeDtypeStruct((rows, wide), jnp.bfloat16)
    square = jax.ShapeDtypeStruct((rows, rows), jnp.bfloat16)
    column = jax.ShapeDtypeStruct((rows, 1), jnp.float32)
    product = 2 * rows * rows * wide

    i1 = swap_image(image_embed)
    t1 = swap_text(text_embed)
    i0_hat, t0_hat = call(own_kernel, "own", [half, half], product, image_embed, text_embed)
    t1, i0_hat, scalars = lax.optimization_barrier((t1, i0_hat, scalars))
    ir = pass_image(i1)
    tr = pass_text(t1)
    i1_hat, t1_hat, inv_i, inv_t, w11, di1, loss1 = call(
        main_kernel, "main", [half, half, column, column, square, full, column], 4 * product,
        scalars, t0_hat, i1, t1,
    )
    (gt1,) = call(
        text_kernel, "text_share", [half], 5 * product,
        scalars, t1, t1_hat, inv_t, ir, i0_hat, i1_hat, w11,
    )
    gt = swap_text(gt1)
    taller = jax.ShapeDtypeStruct((rows + EXTRA, wide), jnp.bfloat16)
    (gi1,) = call(
        image_kernel, "image_share", [taller], 2 * product,
        scalars, i1, i1_hat, inv_i, tr, di1, loss1,
    )
    gi = swap_image(gi1)
    i1_hat, gi1 = lax.optimization_barrier((i1_hat, gi1))
    gi0, gt0, loss0 = call(
        home_kernel, "home", [full, full, column], 7 * product,
        scalars, image_embed, text_embed, i1_hat, t1_hat,
    )
    grad_image, grad_text = call(
        sum_kernel, "total", [half, half], 4 * rows * wide, gi0, gt0, gi, gt
    )
    lines = gi[rows : rows + PIECES, :rows].astype(jnp.float32)
    return (loss0.reshape(rows) + jnp.sum(lines, axis=0), grad_image, grad_text)


def solution(mesh):
    in_specs = (P(("blk", "grp"), None), P(("blk", "grp"), None), P(), P())
    out_specs = (P(("blk", "grp")), P(("blk", "grp"), None), P(("blk", "grp"), None))
    return jax.shard_map(
        on_device, mesh=mesh, in_specs=in_specs, out_specs=out_specs, check_vma=False
    )
```
